128 devices in a mesh: row: 8 (over z, core), col: 16 (over y, x).
Axes of the slice: x: 4, y: 4, z: 4, core: 2. Of those that a mesh axis runs over, the one named last changes fastest.
Arguments:
- normed: bfloat16 [512, 8192], P('row', 'col'), may hold values from -6 to 6
- w_in: bfloat16 [8192, 32768], P('col', 'row'), may hold values from -0.0625 to 0.0625
- w_out: bfloat16 [32768, 8192], P('row', 'col'), may hold values from -0.03125 to 0.03125
- d_out: bfloat16 [512, 8192], P('row', 'col'), may hold values from -6 to 6
Outputs:
- ffn_out: bfloat16 [512, 8192], P('row', 'col')
- d_normed: bfloat16 [512, 8192], P('row', 'col')
- grad_in: bfloat16 [8192, 32768], P('col', 'row')
- grad_out: bfloat16 [32768, 8192], P('row', 'col')
The draws below stay inside these ranges and needn't reach their ends.
All inputs are finite; a program needn't handle non-finite values.
Results may differ from the reference program's by a relative error of at most 0.029.
Values may be sent and summed in bfloat16 or wider, within the bound.
No kernel may reach another device: no remote copies, remote signals or barrier semaphores. Data moves between devices by JAX's collectives and lax.ppermute only.
A program may use at most 128 MiB of HBM per device.

```python
import jax
import jax.numpy as jnp
from jax import lax

D = 8192
FF = 32768
TOKENS = 512
D_BLOCK = 512


def shard_levels(stream_key, extent, shards, smallest, top_value):
    loudness = 1.0
    for position, shards_of in shards:
        draws = jax.random.uniform(jax.random.fold_in(jax.random.fold_in(stream_key, 6), position), (shards_of,), jnp.float32, smallest / len(shards), top_value / len(shards))
        loudness = loudness * jnp.repeat(jnp.exp(draws), extent[position] // shards_of).reshape((-1,) + (1,) * (len(extent) - 1 - position))
    return loudness


def gaussian(stream_key, dims, deviation, reach, shards=(), dtype=jnp.bfloat16):
    entries = jax.random.normal(stream_key, dims, jnp.float32) * deviation
    if len(shards) > 0:
        entries = shard_levels(stream_key, dims, shards, -0.22, 0.18) * entries
    return jnp.clip(entries, min=-reach, max=reach).astype(dtype)


def setup_inputs(seed: int = 0) -> dict:
    streams_of = jax.random.split(jax.random.key(seed), 5)
    return {
        "normed": gaussian(streams_of[0], (TOKENS, D), 1.0, 6.0, ((0, 8), (1, 16))),
        "w_in": gaussian(streams_of[1], (D, FF), D ** -0.5, 0.0625, ((0, 16), (1, 8))),
        "w_out": gaussian(streams_of[2], (FF, D), FF ** -0.5, 0.03125, ((0, 8), (1, 16))),
        "d_out": gaussian(streams_of[3], (TOKENS, D), 1.0, 6.0, ((0, 8), (1, 16))),
    }


def gelu_tanh(value):
    inner = 0.7978845608 * (value + 0.044715 * value * value * value)
    return 0.5 * value * (1.0 + jnp.tanh(inner))


def gelu_slope(value):
    tangent = jnp.tanh(0.7978845608 * (value + 0.044715 * value * value * value))
    return 0.5 * (1.0 + tangent) + 0.5 * value * (1.0 - tangent * tangent) * 0.7978845608 * (1.0 + 3.0 * 0.044715 * value * value)


def blocked_sum(left, right):
    blocks = D // D_BLOCK
    left_blocks = left.reshape(left.shape[0], blocks, D_BLOCK).transpose(1, 0, 2)
    right_blocks = right.reshape(blocks, D_BLOCK, right.shape[1])

    def add_block(carry, pair):
        term = jnp.dot(pair[0], pair[1], preferred_element_type=jnp.float32).astype(jnp.bfloat16)
        term = lax.optimization_barrier(term)
        return carry + term.astype(jnp.float32), None

    start_sum = jnp.zeros((left.shape[0], right.shape[1]), jnp.float32)
    result, unused = lax.scan(add_block, start_sum, (left_blocks, right_blocks))
    return result


def reference(normed, w_in, w_out, d_out):
    preact = blocked_sum(normed, w_in)
    act = gelu_tanh(preact).astype(jnp.bfloat16)
    ffn_out = jnp.dot(act, w_out, preferred_element_type=jnp.float32).astype(jnp.bfloat16)
    d_act = blocked_sum(d_out, jnp.transpose(w_out))
    d_pre = (d_act * gelu_slope(preact)).astype(jnp.bfloat16)
    grad_in = lax.dot_general(normed, d_pre, (((0,), (0,)), ((), ())), preferred_element_type=jnp.float32).astype(jnp.bfloat16)
    grad_out = lax.dot_general(act, d_out, (((0,), (0,)), ((), ())), preferred_element_type=jnp.float32).astype(jnp.bfloat16)
    d_normed = lax.dot_general(d_pre, w_in, (((1,), (1,)), ((), ())), preferred_element_type=jnp.float32).astype(jnp.bfloat16)
    return ffn_out, d_normed, grad_in, grad_out
```

```python
import functools

import jax
import jax.numpy as jnp
from jax import lax
from jax.experimental import pallas as pl
from jax.experimental.pallas import tpu as pltpu
from jax.sharding import PartitionSpec as P

BOTH = ("row", "col")
F32, BF16 = jnp.float32, jnp.bfloat16
WIDE = 256
LIMIT = 48 * 1024 * 1024


def gelu_tanh(value):
    inner = 0.7978845608 * (value + 0.044715 * value * value * value)
    return 0.5 * value * (1.0 + jnp.tanh(inner))


def gelu_slope(value):
    tangent = jnp.tanh(0.7978845608 * (value + 0.044715 * value * value * value))
    return 0.5 * (1.0 + tangent) + 0.5 * value * (1.0 - tangent * tangent) * 0.7978845608 * (
        1.0 + 3.0 * 0.044715 * value * value
    )


GRAY = (0, 1, 3, 2)
UNGRAY = (0, 1, 3, 2)


def pairs(move):
    listed = []
    for z in range(4):
        for core in range(2):
            for y in range(4):
                for x in range(4):
                    tz, tcore, ty, tx = move(z, core, y, x)
                    listed.append(
                        ((z * 2 + core) * 16 + y * 4 + x, (tz * 2 + tcore) * 16 + ty * 4 + tx)
                    )
    return listed


def flip(position, bit):
    return UNGRAY[GRAY[position] ^ (1 << bit)]


PRIMARY = [
    pairs(
        lambda z, core, y, x, bit=bit: (z, core, y, flip(x, bit))
        if core == 0
        else (z, core, flip(y, bit), x)
    )
    for bit in range(2)
]
SECONDARY = [
    pairs(lambda z, core, y, x, k=k: (z, core, y ^ k, x) if core == 0 else (z, core, y, x ^ k))
    for k in range(4)
]
ALONG_Z = [pairs(lambda z, core, y, x, k=k: (z ^ k, core, y, x)) for k in range(4)]
CORES = pairs(lambda z, core, y, x: (z, 1 - core, y, x))


def send(block, perm):
    return lax.ppermute(block, BOTH, perm)


def gray(position):
    return jnp.bitwise_xor(position, jnp.right_shift(position, 1))


def places():
    row, col = lax.axis_index("row"), lax.axis_index("col")
    core, y, x = row % 2, col // 4, col % 4
    primary = gray(jnp.where(core == 0, x, y))
    secondary = jnp.where(core == 0, y, x)
    low, high = primary % 2, primary // 2
    return jnp.stack([low * 8 + high * 4 + secondary, high * 8 + low * 4 + secondary]).astype(
        jnp.int32
    )


def weight_block(transposed, part, first, step, me):
    pair = jnp.bitwise_xor(first + step, jnp.right_shift(me[part], 1)) + 8 * part
    return (pair, 0) if transposed else (0, pair)


def weight_spec(transposed, depth, index):
    return pl.BlockSpec((WIDE, depth) if transposed else (depth, WIDE), index)


def produce_body(transposed, part_of, me, x_ref, w_ref, *outs):
    if transposed:
        term = lax.dot_general(
            x_ref[...], w_ref[...], (((1,), (1,)), ((), ())), preferred_element_type=F32
        )
    else:
        term = jnp.dot(x_ref[...], w_ref[...], preferred_element_type=F32)
    term = term.astype(BF16)

    def put(out, part):
        odd = me[part] % 2
        out[odd] = term[:, : WIDE // 2]
        out[1 - odd] = term[:, WIDE // 2 :]

    if part_of is not None:
        put(outs[0], part_of)
    else:
        for part in range(2):
            pl.when(pl.program_id(0) == part)(functools.partial(put, outs[part], part))


def produce(x, w, me, transposed, part, first):
    tokens, depth = x.shape
    shape = jax.ShapeDtypeStruct((8, tokens, WIDE // 2), BF16)
    block = (2, tokens, WIDE // 2)
    if part is not None:
        grid = (4,)
        w_index = lambda j, me: weight_block(transposed, part, first, j, me)
        x_index = lambda j, me: (0, 0)
        out_specs = [pl.BlockSpec(block, lambda j, me: (j, 0, 0))]
    else:
        grid = (2, 4)
        w_index = lambda i, j, me: weight_block(transposed, i, first, j, me)
        x_index = lambda i, j, me: (0, 0)
        out_specs = [
            pl.BlockSpec(block, lambda i, j, me: (jnp.where(i == 0, j, 3), 0, 0)),
            pl.BlockSpec(block, lambda i, j, me: (jnp.where(i == 0, 0, j), 0, 0)),
        ]
    count = len(out_specs)
    return pl.pallas_call(
        functools.partial(produce_body, transposed, part),
        out_shape=[shape] * count,
        grid_spec=pltpu.PrefetchScalarGridSpec(
            num_scalar_prefetch=1,
            grid=grid,
            in_specs=[
                pl.BlockSpec((tokens, depth), x_index),
                weight_spec(transposed, depth, w_index),
            ],
            out_specs=out_specs,
        ),
        compiler_params=pltpu.CompilerParams(vmem_limit_bytes=LIMIT),
        cost_estimate=pl.CostEstimate(
            flops=2 * tokens * depth * 4 * WIDE * count,
            bytes_accessed=2 * (tokens * depth + 4 * WIDE * (depth + tokens) * count),
            transcendentals=0,
        ),
    )(me, x, w)


def consume_body(transposed, has_total, me, a_ref, b_ref, w_ref, y_ref, *rest):
    if has_total:
        total_in, unused_grad, total, grad = rest
    else:
        total, grad = rest
    i, j = pl.program_id(0), pl.program_id(1)

    @pl.when((i == 0) & (j == 0))
    def start():
        total[...] = total_in[...] if has_total else jnp.zeros_like(total)

    def step(ref, part):
        odd = me[part] % 2
        block = jnp.concatenate([ref[odd], ref[1 - odd]], axis=1)
        if transposed:
            total[...] += jnp.dot(block, w_ref[...], preferred_element_type=F32)
            grad[...] = lax.dot_general(
                block, y_ref[...], (((0,), (0,)), ((), ())), preferred_element_type=F32
            ).astype(BF16)
        else:
            total[...] += lax.dot_general(
                block, w_ref[...], (((1,), (1,)), ((), ())), preferred_element_type=F32
            )
            grad[...] = jnp.dot(y_ref[...], block, preferred_element_type=F32).astype(BF16)

    for part, ref in enumerate((a_ref, b_ref)):
        pl.when(i == part)(functools.partial(step, ref, part))


def consume(a, b, w, y, me, transposed, first, before):
    tokens, depth = y.shape
    block = (2, tokens, WIDE // 2)
    w_index = lambda i, j, me: weight_block(transposed, i, first, j, me)
    whole = lambda i, j, me: (0, 0)
    in_specs = [
        pl.BlockSpec(block, lambda i, j, me: (jnp.where(i == 0, j, 3), 0, 0)),
        pl.BlockSpec(block, lambda i, j, me: (jnp.where(i == 0, 0, j), 0, 0)),
        weight_spec(transposed, depth, w_index),
        pl.BlockSpec(y.shape, whole),
    ]
    operands = [me, a, b, w, y]
    aliases = {}
    if before is not None:
        in_specs += [pl.BlockSpec((tokens, depth), whole), pl.BlockSpec(memory_space=pl.ANY)]
        operands += list(before)
        aliases = {5: 0, 6: 1}
    return pl.pallas_call(
        functools.partial(consume_body, transposed, before is not None),
        out_shape=[
            jax.ShapeDtypeStruct((tokens, depth), F32),
            jax.ShapeDtypeStruct(w.shape, BF16),
        ],
        grid_spec=pltpu.PrefetchScalarGridSpec(
            num_scalar_prefetch=1,
            grid=(2, 4),
            in_specs=in_specs,
            out_specs=[
                pl.BlockSpec((tokens, depth), whole),
                weight_spec(transposed, depth, w_index),
            ],
        ),
        input_output_aliases=aliases,
        compiler_params=pltpu.CompilerParams(vmem_limit_bytes=LIMIT),
        cost_estimate=pl.CostEstimate(
            flops=4 * tokens * depth * 8 * WIDE,
            bytes_accessed=2 * (3 * tokens * depth + 8 * WIDE * (2 * depth + tokens)),
            transcendentals=0,
        ),
    )(*operands)


def add(*terms):
    total = terms[0].astype(F32)
    for term in terms[1:]:
        total = total + term.astype(F32)
    return total


def gather_rows(block):
    along = jnp.concatenate([block] + [send(block, ALONG_Z[k]) for k in (1, 3, 2)], axis=0)
    return jnp.concatenate([along, send(along, CORES)], axis=0)


def scatter_rows(total):
    half = total.shape[0] // 2
    other = send(total[half:].astype(BF16), CORES)
    kept = add(total[:half], other)
    rows = half // 4
    sent = [kept[rows * n : rows * (n + 1)].astype(BF16) for n in range(1, 4)]
    got = [send(sent[n], ALONG_Z[k]) for n, k in enumerate((1, 3, 2))]
    return add(kept[:rows], *got).astype(BF16)


def reduce_hidden(x, w, me, transposed):
    (far_a,) = produce(x, w, me, transposed, 0, 4)
    got_a = send(far_a, PRIMARY[0])
    (far_b,) = produce(x, w, me, transposed, 1, 4)
    got_b = send(far_b, PRIMARY[1])
    near_a, near_b = produce(x, w, me, transposed, None, 0)
    next_a = send(add(near_a[4:], got_a[4:]).astype(BF16), PRIMARY[1])
    next_b = send(add(near_b[4:], got_b[4:]).astype(BF16), PRIMARY[0])
    four_a = add(near_a[:4], got_a[:4], next_a)
    four_b = add(near_b[:4], got_b[:4], next_b)
    own = jnp.stack([four_a[0], four_b[0]])
    last = [
        send(jnp.stack([four_a[k], four_b[k]]).astype(BF16), SECONDARY[k]) for k in (1, 3, 2)
    ]
    return add(own, *last)


def spread_hidden(own):
    one, three, two = (send(own, SECONDARY[k]) for k in (1, 3, 2))
    four = [jnp.stack([own[h], one[h], two[h], three[h]]) for h in range(2)]
    near = [
        jnp.concatenate([four[h], send(four[h], PRIMARY[1 - h])], axis=0) for h in range(2)
    ]
    far = [send(near[h], PRIMARY[h]) for h in range(2)]
    return near, far


def shards(normed, w_in, w_out, d_out):
    me = places()
    inputs = gather_rows(normed)
    cotangent = gather_rows(d_out)
    preact = reduce_hidden(inputs, w_in, me, False)
    act = gelu_tanh(preact).astype(BF16)
    d_act = reduce_hidden(cotangent, w_out, me, True)
    near, far = spread_hidden(act)
    d_pre = (d_act * gelu_slope(preact)).astype(BF16)
    d_near, d_far = spread_hidden(d_pre)
    first = consume(near[0], near[1], w_out, cotangent, me, True, 0, None)
    ffn_total, grad_out = consume(far[0], far[1], w_out, cotangent, me, True, 4, first)
    ffn_out = scatter_rows(ffn_total)
    turned = inputs.T
    first = consume(d_near[0], d_near[1], w_in, turned, me, False, 0, None)
    d_total, grad_in = consume(d_far[0], d_far[1], w_in, turned, me, False, 4, first)
    d_normed = scatter_rows(d_total)
    return (ffn_out, d_normed, grad_in, grad_out)


def solution(mesh):
    return jax.shard_map(
        shards,
        mesh=mesh,
        in_specs=(P("row", "col"), P("col", "row"), P("row", "col"), P("row", "col")),
        out_specs=(P("row", "col"), P("row", "col"), P("col", "row"), P("row", "col")),
        check_vma=False,
    )
```

```python
import functools

import jax
import jax.numpy as jnp
from jax import lax
from jax.experimental import pallas as pl
from jax.experimental.pallas import tpu as pltpu
from jax.sharding import PartitionSpec as P

BOTH = ("row", "col")
F32, BF16 = jnp.float32, jnp.bfloat16
CHUNK = 128
EIGHT = 8
LIMIT = 20 * 1024 * 1024


def gelu_tanh(value):
    inner = 0.7978845608 * (value + 0.044715 * value * value * value)
    return 0.5 * value * (1.0 + jnp.tanh(inner))


def gelu_slope(value):
    tangent = jnp.tanh(0.7978845608 * (value + 0.044715 * value * value * value))
    return 0.5 * (1.0 + tangent) + 0.5 * value * (1.0 - tangent * tangent) * 0.7978845608 * (
        1.0 + 3.0 * 0.044715 * value * value
    )


GRAY = (0, 1, 3, 2)
UNGRAY = (0, 1, 3, 2)


def pairs(move):
    listed = []
    for z in range(4):
        for core in range(2):
            for y in range(4):
                for x in range(4):
                    tz, tcore, ty, tx = move(z, core, y, x)
                    listed.append(
                        ((z * 2 + core) * 16 + y * 4 + x, (tz * 2 + tcore) * 16 + ty * 4 + tx)
                    )
    return listed


def flip(position, bit):
    return UNGRAY[GRAY[position] ^ (1 << bit)]


PRIMARY = [
    pairs(
        lambda z, core, y, x, bit=bit: (z, core, y, flip(x, bit))
        if core == 0
        else (z, core, flip(y, bit), x)
    )
    for bit in range(2)
]
SECONDARY = [
    pairs(lambda z, core, y, x, k=k: (z, core, y ^ k, x) if core == 0 else (z, core, y, x ^ k))
    for k in range(4)
]
FIRST_Z, SECOND_Z = (
    pairs(lambda z, core, y, x, turn=turn: (flip(z, core ^ turn), core, y, x)) for turn in range(2)
)
ACROSS_Z = pairs(lambda z, core, y, x: (z ^ 2, core, y, x))
CORES = pairs(lambda z, core, y, x: (z, 1 - core, y, x))


def send(block, perm):
    return lax.ppermute(block, BOTH, perm)


def gray(position):
    return jnp.bitwise_xor(position, jnp.right_shift(position, 1))


def places():
    row, col = lax.axis_index("row"), lax.axis_index("col")
    core, y, x = row % 2, col // 4, col % 4
    primary = gray(jnp.where(core == 0, x, y))
    secondary = jnp.where(core == 0, y, x)
    low, high = primary % 2, primary // 2
    return jnp.stack([low * 8 + high * 4 + secondary, high * 8 + low * 4 + secondary]).astype(
        jnp.int32
    )


def order(me, part, count):
    return [jnp.bitwise_xor(chunk, me[part] % count) for chunk in range(count)]


def weight_spec(transposed, depth, first, part_of):
    def index(i, me):
        part = part_of(i)
        group = jnp.bitwise_xor(first, jnp.right_shift(me[part], 3)) + 2 * part
        return (group, 0) if transposed else (0, group)

    wide = EIGHT * CHUNK
    return pl.BlockSpec((wide, depth) if transposed else (depth, wide), index)


def produce_body(transposed, parts, me, x_ref, w_ref, *outs):
    if transposed:
        term = lax.dot_general(
            x_ref[...], w_ref[...], (((1,), (1,)), ((), ())), preferred_element_type=F32
        )
    else:
        term = jnp.dot(x_ref[...], w_ref[...], preferred_element_type=F32)
    term = term.astype(BF16)

    def put(out, part):
        for chunk, place in enumerate(order(me, part, EIGHT)):
            out[place] = term[:, CHUNK * chunk : CHUNK * (chunk + 1)]

    if len(parts) == 1:
        put(outs[0], parts[0])
    else:
        for n, part in enumerate(parts):
            pl.when(pl.program_id(0) == n)(functools.partial(put, outs[n], part))


def produce(x, w, me, transposed, parts, first):
    tokens, depth = x.shape
    count = len(parts)
    part_of = (lambda i: parts[0]) if count == 1 else (lambda i: i)
    block = (EIGHT, tokens, CHUNK)
    return pl.pallas_call(
        functools.partial(produce_body, transposed, parts),
        out_shape=[jax.ShapeDtypeStruct(block, BF16)] * count,
        grid_spec=pltpu.PrefetchScalarGridSpec(
            num_scalar_prefetch=1,
            grid=(count,),
            in_specs=[
                pl.BlockSpec((tokens, depth), lambda i, me: (0, 0)),
                weight_spec(transposed, depth, first, part_of),
            ],
            out_specs=[pl.BlockSpec(block, lambda i, me: (0, 0, 0))] * count,
        ),
        compiler_params=pltpu.CompilerParams(vmem_limit_bytes=LIMIT),
        cost_estimate=pl.CostEstimate(
            flops=tokens * depth * CHUNK * count,
            bytes_accessed=tokens * depth,
            transcendentals=0,
        ),
    )(me, x, w)


def consume_body(transposed, has_total, has_grad, wants, me, a_ref, b_ref, *rest):
    rest = list(rest)
    w_ref = rest.pop(0) if "total" in wants else None
    y_ref = rest.pop(0) if "grad" in wants else None
    total_in = rest.pop(0) if has_total else None
    if has_grad:
        rest.pop(0)
    total = rest.pop(0) if "total" in wants else None
    grad = rest.pop(0) if "grad" in wants else None

    def step(ref, part):
        block = jnp.concatenate([ref[place] for place in order(me, part, EIGHT)], axis=1)
        if grad is not None and transposed:
            grad[...] = lax.dot_general(
                block, y_ref[...], (((0,), (0,)), ((), ())), preferred_element_type=F32
            ).astype(BF16)
        elif grad is not None:
            grad[...] = jnp.dot(y_ref[...], block, preferred_element_type=F32).astype(BF16)
        if total is not None:
            dims = ((1,), (0,)) if transposed else ((1,), (1,))
            added = lax.dot_general(block, w_ref[...], (dims, ((), ())), preferred_element_type=F32)
            if part == 1:
                total[...] += added
            elif has_total:
                total[...] = total_in[...] + added
            else:
                total[...] = added

    for part, ref in enumerate((a_ref, b_ref)):
        pl.when(pl.program_id(0) == part)(functools.partial(step, ref, part))


def consume(a, b, w, y, me, transposed, first, total=None, grad=None, wants=("total", "grad")):
    tokens, depth = y.shape
    block = (EIGHT, tokens, CHUNK)
    whole = lambda i, me: (0, 0)
    chunks = pl.BlockSpec(block, lambda i, me: (0, 0, 0))
    weights = weight_spec(transposed, depth, first, lambda i: i)
    in_specs, operands = [chunks, chunks], [me, a, b]
    out_specs, out_shape, aliases = [], [], {}
    if "total" in wants:
        in_specs.append(weights)
        operands.append(w)
        out_specs.append(pl.BlockSpec((tokens, depth), whole))
        out_shape.append(jax.ShapeDtypeStruct((tokens, depth), F32))
    if "grad" in wants:
        in_specs.append(pl.BlockSpec(y.shape, whole))
        operands.append(y)
        out_specs.append(weights)
        out_shape.append(jax.ShapeDtypeStruct(w.shape, BF16))
    if total is not None:
        aliases[len(operands)] = 0
        in_specs.append(pl.BlockSpec((tokens, depth), whole))
        operands.append(total)
    if grad is not None:
        aliases[len(operands)] = len(out_shape) - 1
        in_specs.append(pl.BlockSpec(memory_space=pl.ANY))
        operands.append(grad)
    return pl.pallas_call(
        functools.partial(consume_body, transposed, total is not None, grad is not None, wants),
        out_shape=out_shape,
        grid_spec=pltpu.PrefetchScalarGridSpec(
            num_scalar_prefetch=1, grid=(2,), in_specs=in_specs, out_specs=out_specs
        ),
        input_output_aliases=aliases,
        compiler_params=pltpu.CompilerParams(vmem_limit_bytes=LIMIT),
        cost_estimate=pl.CostEstimate(
            flops=4 * tokens * depth * CHUNK,
            bytes_accessed=tokens * depth,
            transcendentals=0,
        ),
    )(*operands)


def add(*terms):
    total = terms[0].astype(F32)
    for term in terms[1:]:
        total = total + term.astype(F32)
    return total


def after(value, *others):
    return lax.optimization_barrier((value,) + others)[0]


def join(block, got):
    return jnp.concatenate([block, got], axis=0)


def gather_rows(normed, d_out):
    normed = join(normed, send(normed, FIRST_Z))
    d_out = join(d_out, send(d_out, FIRST_Z))
    normed = join(normed, send(normed, SECOND_Z))
    d_out = join(d_out, send(after(d_out, normed), SECOND_Z))
    normed = join(normed, send(normed, CORES))
    d_out = join(d_out, send(d_out, CORES))
    return normed, d_out


def scatter_rows(total):
    half = total.shape[0] // 2
    total = add(total[:half], send(total[half:].astype(BF16), CORES))
    rows = half // 4
    parts = [total[rows * n : rows * (n + 1)] for n in range(4)]
    got = [send(parts[n].astype(BF16), perm) for n, perm in ((1, FIRST_Z), (2, SECOND_Z), (3, ACROSS_Z))]
    return add(parts[0], *got).astype(BF16)


def halve_first(x, w, me, transposed):
    far = [produce(x, w, me, transposed, (h,), 1)[0] for h in range(2)]
    got = [send(far[h], PRIMARY[h]) for h in range(2)]
    near = produce(x, w, me, transposed, (0, 1), 0)
    return near, got


def halve_second(near, got):
    out = [send(add(near[h][4:], got[h][4:]).astype(BF16), PRIMARY[1 - h]) for h in range(2)]
    return [add(near[h][:4], got[h][:4], out[h]) for h in range(2)]


def exchange(four):
    own = jnp.stack([four[0][0], four[1][0]])
    last = [
        send(jnp.stack([four[0][k], four[1][k]]).astype(BF16), SECONDARY[k]) for k in (1, 3, 2)
    ]
    return add(own, *last)


def spread_first(own):
    one, three, two = (send(own, SECONDARY[k]) for k in (1, 3, 2))
    return [jnp.stack([own[h], one[h], two[h], three[h]]) for h in range(2)]


def spread_second(four):
    return [
        jnp.concatenate([four[h], send(four[h], PRIMARY[1 - h])], axis=0) for h in range(2)
    ]


def spread_third(near):
    return [send(near[h], PRIMARY[h]) for h in range(2)]


def shards(normed, w_in, w_out, d_out):
    me = places()
    inputs, cotangent = gather_rows(normed, d_out)
    turned = inputs.T
    p_near, p_got = halve_first(inputs, w_in, me, False)
    d_near, d_got = halve_first(cotangent, w_out, me, True)
    p_four = halve_second(p_near, p_got)
    d_four = halve_second(d_near, d_got)
    preact = exchange(p_four)
    d_act = exchange(d_four)
    act = gelu_tanh(preact).astype(BF16)
    act, preact = lax.optimization_barrier((act, preact))
    p_four = spread_first(act)
    d_pre = (d_act * gelu_slope(preact)).astype(BF16)
    p_near = spread_second(p_four)
    d_four = spread_first(after(d_pre, *p_four))
    p_far = spread_third(p_near)
    d_near = spread_second([after(d_four[h], p_near[h]) for h in range(2)])
    total, grad = consume(p_near[0], p_near[1], w_out, cotangent, me, True, 0)
    d_far = spread_third([after(d_near[h], total) for h in range(2)])
    d_total, d_grad = consume(d_near[0], d_near[1], w_in, turned, me, False, 0)
    p_far[0] = after(p_far[0], d_total)
    total, grad_out = consume(p_far[0], p_far[1], w_out, cotangent, me, True, 1, total, grad)
    ffn_out = scatter_rows(total)
    (d_total,) = consume(d_far[0], d_far[1], w_in, turned, me, False, 1, d_total, None, ("total",))
    d_normed = scatter_rows(d_total)
    (grad_in,) = consume(
        after(d_far[0], d_total), d_far[1], w_in, turned, me, False, 1, None, d_grad, ("grad",)
    )
    return (ffn_out, d_normed, grad_in, grad_out)


def solution(mesh):
    return jax.shard_map(
        shards,
        mesh=mesh,
        in_specs=(P("row", "col"), P("col", "row"), P("row", "col"), P("row", "col")),
        out_specs=(P("row", "col"), P("row", "col"), P("col", "row"), P("row", "col")),
        check_vma=False,
    )
```

```python
import functools

import jax
import jax.numpy as jnp
from jax import lax
from jax.experimental import pallas as pl
from jax.experimental.pallas import tpu as pltpu
from jax.sharding import PartitionSpec as P

BOTH = ("row", "col")
F32, BF16 = jnp.float32, jnp.bfloat16
CHUNK = 128
EIGHT = 8
LIMIT = 20 * 1024 * 1024


def gelu_tanh(value):
    inner = 0.7978845608 * (value + 0.044715 * value * value * value)
    return 0.5 * value * (1.0 + jnp.tanh(inner))


def gelu_slope(value):
    tangent = jnp.tanh(0.7978845608 * (value + 0.044715 * value * value * value))
    return 0.5 * (1.0 + tangent) + 0.5 * value * (1.0 - tangent * tangent) * 0.7978845608 * (
        1.0 + 3.0 * 0.044715 * value * value
    )


GRAY = (0, 1, 3, 2)
UNGRAY = (0, 1, 3, 2)


def pairs(move):
    listed = []
    for z in range(4):
        for core in range(2):
            for y in range(4):
                for x in range(4):
                    tz, tcore, ty, tx = move(z, core, y, x)
                    listed.append(
                        ((z * 2 + core) * 16 + y * 4 + x, (tz * 2 + tcore) * 16 + ty * 4 + tx)
                    )
    return listed


def flip(position, bit):
    return UNGRAY[GRAY[position] ^ (1 << bit)]


PRIMARY = [
    pairs(
        lambda z, core, y, x, bit=bit: (z, core, y, flip(x, bit))
        if core == 0
        else (z, core, flip(y, bit), x)
    )
    for bit in range(2)
]
SECONDARY = [
    pairs(lambda z, core, y, x, k=k: (z, core, y ^ k, x) if core == 0 else (z, core, y, x ^ k))
    for k in range(4)
]
FIRST_Z, SECOND_Z = (
    pairs(lambda z, core, y, x, turn=turn: (flip(z, core ^ turn), core, y, x)) for turn in range(2)
)
ACROSS_Z = pairs(lambda z, core, y, x: (z ^ 2, core, y, x))
CORES = pairs(lambda z, core, y, x: (z, 1 - core, y, x))


def send(block, perm):
    return lax.ppermute(block, BOTH, perm)


def gray(position):
    return jnp.bitwise_xor(position, jnp.right_shift(position, 1))


def places():
    row, col = lax.axis_index("row"), lax.axis_index("col")
    core, y, x = row % 2, col // 4, col % 4
    primary = gray(jnp.where(core == 0, x, y))
    secondary = jnp.where(core == 0, y, x)
    low, high = primary % 2, primary // 2
    return jnp.stack([low * 8 + high * 4 + secondary, high * 8 + low * 4 + secondary]).astype(
        jnp.int32
    )


def order(me, part, count):
    return [jnp.bitwise_xor(chunk, me[part] % count) for chunk in range(count)]


def weight_spec(transposed, depth, first, part_of):
    def index(i, me):
        part = part_of(i)
        group = jnp.bitwise_xor(first, jnp.right_shift(me[part], 3)) + 2 * part
        return (group, 0) if transposed else (0, group)

    wide = EIGHT * CHUNK
    return pl.BlockSpec((wide, depth) if transposed else (depth, wide), index)


def produce_body(transposed, parts, me, x_ref, w_ref, *outs):
    if transposed:
        term = lax.dot_general(
            x_ref[...], w_ref[...], (((1,), (1,)), ((), ())), preferred_element_type=F32
        )
    else:
        term = jnp.dot(x_ref[...], w_ref[...], preferred_element_type=F32)
    term = term.astype(BF16)

    def put(out, part):
        for chunk, place in enumerate(order(me, part, EIGHT)):
            out[place] = term[:, CHUNK * chunk : CHUNK * (chunk + 1)]

    if len(parts) == 1:
        put(outs[0], parts[0])
    else:
        for n, part in enumerate(parts):
            pl.when(pl.program_id(0) == n)(functools.partial(put, outs[n], part))


def produce(x, w, me, transposed, parts, first):
    tokens, depth = x.shape
    count = len(parts)
    part_of = (lambda i: parts[0]) if count == 1 else (lambda i: i)
    block = (EIGHT, tokens, CHUNK)
    return pl.pallas_call(
        functools.partial(produce_body, transposed, parts),
        out_shape=[jax.ShapeDtypeStruct(block, BF16)] * count,
        grid_spec=pltpu.PrefetchScalarGridSpec(
            num_scalar_prefetch=1,
            grid=(count,),
            in_specs=[
                pl.BlockSpec((tokens, depth), lambda i, me: (0, 0)),
                weight_spec(transposed, depth, first, part_of),
            ],
            out_specs=[pl.BlockSpec(block, lambda i, me: (0, 0, 0))] * count,
        ),
        compiler_params=pltpu.CompilerParams(vmem_limit_bytes=LIMIT),
        cost_estimate=pl.CostEstimate(
            flops=tokens * depth * CHUNK * count,
            bytes_accessed=tokens * depth,
            transcendentals=0,
        ),
    )(me, x, w)


def consume_body(transposed, has_total, has_grad, wants, me, a_ref, b_ref, *rest):
    rest = list(rest)
    w_ref = rest.pop(0) if "total" in wants else None
    y_ref = rest.pop(0) if "grad" in wants else None
    total_in = rest.pop(0) if has_total else None
    if has_grad:
        rest.pop(0)
    total = rest.pop(0) if "total" in wants else None
    grad = rest.pop(0) if "grad" in wants else None

    def step(ref, part):
        block = jnp.concatenate([ref[place] for place in order(me, part, EIGHT)], axis=1)
        if grad is not None and transposed:
            grad[...] = lax.dot_general(
                block, y_ref[...], (((0,), (0,)), ((), ())), preferred_element_type=F32
            ).astype(BF16)
        elif grad is not None:
            grad[...] = lax.dot_general(
                y_ref[...], block, (((0,), (0,)), ((), ())), preferred_element_type=F32
            ).astype(BF16)
        if total is not None:
            dims = ((1,), (0,)) if transposed else ((1,), (1,))
            added = lax.dot_general(block, w_ref[...], (dims, ((), ())), preferred_element_type=F32)
            if part == 1:
                total[...] += added
            elif has_total:
                total[...] = total_in[...] + added
            else:
                total[...] = added

    for part, ref in enumerate((a_ref, b_ref)):
        pl.when(pl.program_id(0) == part)(functools.partial(step, ref, part))


def consume(a, b, w, y, me, transposed, first, total=None, grad=None, wants=("total", "grad")):
    tokens, depth = y.shape
    block = (EIGHT, tokens, CHUNK)
    whole = lambda i, me: (0, 0)
    chunks = pl.BlockSpec(block, lambda i, me: (0, 0, 0))
    weights = weight_spec(transposed, depth, first, lambda i: i)
    in_specs, operands = [chunks, chunks], [me, a, b]
    out_specs, out_shape, aliases = [], [], {}
    if "total" in wants:
        in_specs.append(weights)
        operands.append(w)
        out_specs.append(pl.BlockSpec((tokens, depth), whole))
        out_shape.append(jax.ShapeDtypeStruct((tokens, depth), F32))
    if "grad" in wants:
        in_specs.append(pl.BlockSpec(y.shape, whole))
        operands.append(y)
        out_specs.append(weights)
        out_shape.append(jax.ShapeDtypeStruct(w.shape, BF16))
    if total is not None:
        aliases[len(operands)] = 0
        in_specs.append(pl.BlockSpec((tokens, depth), whole))
        operands.append(total)
    if grad is not None:
        aliases[len(operands)] = len(out_shape) - 1
        in_specs.append(pl.BlockSpec(memory_space=pl.ANY))
        operands.append(grad)
    return pl.pallas_call(
        functools.partial(consume_body, transposed, total is not None, grad is not None, wants),
        out_shape=out_shape,
        grid_spec=pltpu.PrefetchScalarGridSpec(
            num_scalar_prefetch=1, grid=(2,), in_specs=in_specs, out_specs=out_specs
        ),
        input_output_aliases=aliases,
        compiler_params=pltpu.CompilerParams(vmem_limit_bytes=LIMIT),
        cost_estimate=pl.CostEstimate(
            flops=4 * tokens * depth * CHUNK,
            bytes_accessed=tokens * depth,
            transcendentals=0,
        ),
    )(*operands)


def add(*terms):
    total = terms[0].astype(F32)
    for term in terms[1:]:
        total = total + term.astype(F32)
    return total


def after(value, *others):
    return lax.optimization_barrier((value,) + others)[0]


def join(block, got):
    return jnp.concatenate([block, got], axis=0)


def gather_rows(normed, d_out):
    normed = join(normed, send(normed, FIRST_Z))
    d_out = join(d_out, send(d_out, FIRST_Z))
    normed = join(normed, send(normed, SECOND_Z))
    got = send(after(d_out, normed), SECOND_Z)
    normed = join(normed, send(normed, CORES))
    return normed, (d_out, got)


def stage(values, *earlier):
    values, unused = lax.optimization_barrier((values, earlier))
    return values


def fuse(blocks):
    blocks = [block.astype(BF16) for block in blocks]
    return blocks[0] if len(blocks) == 1 else jnp.stack(blocks)


def split(block, count):
    return [block] if count == 1 else [block[n] for n in range(count)]


def scatter_rows(totals):
    count = len(totals)
    half = totals[0].shape[0] // 2
    got = split(send(fuse([total[half:] for total in totals]), CORES), count)
    totals = [add(total[:half], other) for total, other in zip(totals, got)]
    rows = half // 4
    kept = [total[:rows] for total in totals]
    sent = [fuse([total[rows * n : rows * (n + 1)] for total in totals]) for n in range(1, 4)]
    got = [
        split(send(block, perm), count)
        for block, perm in zip(sent, (FIRST_Z, SECOND_Z, ACROSS_Z))
    ]
    return [add(kept[n], *[g[n] for g in got]).astype(BF16) for n in range(count)], sent


def halve_first(x, w, me, transposed):
    far = [produce(x, w, me, transposed, (h,), 1)[0] for h in range(2)]
    got = [send(far[h], PRIMARY[h]) for h in range(2)]
    near = produce(x, w, me, transposed, (0, 1), 0)
    return near, got


def halve_second(near, got):
    out = [send(add(near[h][4:], got[h][4:]).astype(BF16), PRIMARY[1 - h]) for h in range(2)]
    return [add(near[h][:4], got[h][:4], out[h]) for h in range(2)]


def exchange(four):
    own = jnp.stack([four[0][0], four[1][0]])
    last = [
        send(jnp.stack([four[0][k], four[1][k]]).astype(BF16), SECONDARY[k]) for k in (1, 3, 2)
    ]
    return add(own, *last)


def spread_first(own):
    one, three, two = (send(own, SECONDARY[k]) for k in (1, 3, 2))
    return [jnp.stack([own[h], one[h], two[h], three[h]]) for h in range(2)]


def spread_second(four):
    return [
        jnp.concatenate([four[h], send(four[h], PRIMARY[1 - h])], axis=0) for h in range(2)
    ]


def spread_third(near):
    return [send(near[h], PRIMARY[h]) for h in range(2)]


def shards(normed, w_in, w_out, d_out):
    me = places()
    inputs, rows = gather_rows(normed, d_out)
    p_out = [produce(inputs, w_in, me, False, (0,), 1)[0]]
    cotangent = join(*rows)
    cotangent = join(cotangent, send(cotangent, CORES))
    p_out.append(produce(inputs, w_in, me, False, (1,), 1)[0])
    p_got = [send(p_out[h], PRIMARY[h]) for h in range(2)]
    p_near = produce(inputs, w_in, me, False, (0, 1), 0)
    d_near, d_got = halve_first(cotangent, w_out, me, True)
    p_four = halve_second(p_near, p_got)
    d_four = halve_second(d_near, d_got)
    preact = exchange(p_four)
    d_act = exchange(d_four)
    act = gelu_tanh(preact).astype(BF16)
    act, preact = lax.optimization_barrier((act, preact))
    p_four = spread_first(act)
    d_pre = (d_act * gelu_slope(preact)).astype(BF16)
    p_near = spread_second(p_four)
    d_four = spread_first(d_pre)
    p_far = spread_third(p_near)
    d_near = spread_second([after(d_four[h], p_near[h]) for h in range(2)])
    total, grad = consume(p_near[0], p_near[1], w_out, cotangent, me, True, 0)
    d_far = spread_third([after(d_near[h], total) for h in range(2)])
    d_total, d_grad = consume(d_near[0], d_near[1], w_in, inputs, me, False, 0)
    p_far[0] = after(p_far[0], d_total)
    total, grad_out = consume(p_far[0], p_far[1], w_out, cotangent, me, True, 1, total, grad)
    (d_total,) = consume(d_far[0], d_far[1], w_in, inputs, me, False, 1, d_total, None, ("total",))
    (ffn_out, d_normed), sent = scatter_rows([total, d_total])
    d_far = stage(d_far, d_total, sent)
    (grad_in,) = consume(d_far[0], d_far[1], w_in, inputs, me, False, 1, None, d_grad, ("grad",))
    return (ffn_out, d_normed, grad_in, grad_out)


def solution(mesh):
    return jax.shard_map(
        shards,
        mesh=mesh,
        in_specs=(P("row", "col"), P("col", "row"), P("row", "col"), P("row", "col")),
        out_specs=(P("row", "col"), P("row", "col"), P("col", "row"), P("row", "col")),
        check_vma=False,
    )
```

```python
import functools

import jax
import jax.numpy as jnp
from jax import lax
from jax.experimental import pallas as pl
from jax.experimental.pallas import tpu as pltpu
from jax.sharding import PartitionSpec as P

BOTH = ("row", "col")
F32, BF16 = jnp.float32, jnp.bfloat16
CHUNK = 128
EIGHT = 8
LIMIT = 20 * 1024 * 1024


def gelu_tanh(value):
    inner = 0.7978845608 * (value + 0.044715 * value * value * value)
    return 0.5 * value * (1.0 + jnp.tanh(inner))


def gelu_slope(value):
    tangent = jnp.tanh(0.7978845608 * (value + 0.044715 * value * value * value))
    return 0.5 * (1.0 + tangent) + 0.5 * value * (1.0 - tangent * tangent) * 0.7978845608 * (
        1.0 + 3.0 * 0.044715 * value * value
    )


GRAY = (0, 1, 3, 2)
UNGRAY = (0, 1, 3, 2)


def pairs(move):
    listed = []
    for z in range(4):
        for core in range(2):
            for y in range(4):
                for x in range(4):
                    tz, tcore, ty, tx = move(z, core, y, x)
                    listed.append(
                        ((z * 2 + core) * 16 + y * 4 + x, (tz * 2 + tcore) * 16 + ty * 4 + tx)
                    )
    return listed


def flip(position, bit):
    return UNGRAY[GRAY[position] ^ (1 << bit)]


PRIMARY = [
    pairs(
        lambda z, core, y, x, bit=bit: (z, core, y, flip(x, bit))
        if core == 0
        else (z, core, flip(y, bit), x)
    )
    for bit in range(2)
]
SECONDARY = [
    pairs(lambda z, core, y, x, k=k: (z, core, y ^ k, x) if core == 0 else (z, core, y, x ^ k))
    for k in range(4)
]
FIRST_Z, SECOND_Z = (
    pairs(lambda z, core, y, x, turn=turn: (flip(z, core ^ turn), core, y, x)) for turn in range(2)
)
ACROSS_Z = pairs(lambda z, core, y, x: (z ^ 2, core, y, x))
CORES = pairs(lambda z, core, y, x: (z, 1 - core, y, x))


def send(block, perm):
    return lax.ppermute(block, BOTH, perm)


def gray(position):
    return jnp.bitwise_xor(position, jnp.right_shift(position, 1))


def places():
    row, col = lax.axis_index("row"), lax.axis_index("col")
    core, y, x = row % 2, col // 4, col % 4
    primary = gray(jnp.where(core == 0, x, y))
    secondary = jnp.where(core == 0, y, x)
    low, high = primary % 2, primary // 2
    return jnp.stack([low * 8 + high * 4 + secondary, high * 8 + low * 4 + secondary]).astype(
        jnp.int32
    )


def order(me, part, count):
    return [jnp.bitwise_xor(chunk, me[part] % count) for chunk in range(count)]


def weight_spec(transposed, depth, first, part_of):
    def index(i, me):
        part = part_of(i)
        group = jnp.bitwise_xor(first, jnp.right_shift(me[part], 3)) + 2 * part
        return (group, 0) if transposed else (0, group)

    wide = EIGHT * CHUNK
    return pl.BlockSpec((wide, depth) if transposed else (depth, wide), index)


def produce_body(transposed, parts, me, x_ref, w_ref, *outs):
    if transposed:
        term = lax.dot_general(
            x_ref[...], w_ref[...], (((1,), (1,)), ((), ())), preferred_element_type=F32
        )
    else:
        term = jnp.dot(x_ref[...], w_ref[...], preferred_element_type=F32)
    term = term.astype(BF16)

    def put(out, part):
        for chunk, place in enumerate(order(me, part, EIGHT)):
            out[place] = term[:, CHUNK * chunk : CHUNK * (chunk + 1)]

    if len(parts) == 1:
        put(outs[0], parts[0])
    else:
        for n, part in enumerate(parts):
            pl.when(pl.program_id(0) == n)(functools.partial(put, outs[n], part))


def produce(x, w, me, transposed, parts, first):
    tokens, depth = x.shape
    count = len(parts)
    part_of = (lambda i: parts[0]) if count == 1 else (lambda i: i)
    block = (EIGHT, tokens, CHUNK)
    return pl.pallas_call(
        functools.partial(produce_body, transposed, parts),
        out_shape=[jax.ShapeDtypeStruct(block, BF16)] * count,
        grid_spec=pltpu.PrefetchScalarGridSpec(
            num_scalar_prefetch=1,
            grid=(count,),
            in_specs=[
                pl.BlockSpec((tokens, depth), lambda i, me: (0, 0)),
                weight_spec(transposed, depth, first, part_of),
            ],
            out_specs=[pl.BlockSpec(block, lambda i, me: (0, 0, 0))] * count,
        ),
        compiler_params=pltpu.CompilerParams(vmem_limit_bytes=LIMIT),
        cost_estimate=pl.CostEstimate(
            flops=tokens * depth * CHUNK * count,
            bytes_accessed=tokens * depth,
            transcendentals=0,
        ),
    )(me, x, w)


def consume_body(transposed, has_total, has_grad, wants, me, a_ref, b_ref, *rest):
    rest = list(rest)
    w_ref = rest.pop(0) if "total" in wants else None
    y_ref = rest.pop(0) if "grad" in wants else None
    total_in = rest.pop(0) if has_total else None
    if has_grad:
        rest.pop(0)
    total = rest.pop(0) if "total" in wants else None
    grad = rest.pop(0) if "grad" in wants else None

    def step(ref, part):
        block = jnp.concatenate([ref[place] for place in order(me, part, EIGHT)], axis=1)
        if grad is not None and transposed:
            grad[...] = lax.dot_general(
                block, y_ref[...], (((0,), (0,)), ((), ())), preferred_element_type=F32
            ).astype(BF16)
        elif grad is not None:
            grad[...] = lax.dot_general(
                y_ref[...], block, (((0,), (0,)), ((), ())), preferred_element_type=F32
            ).astype(BF16)
        if total is not None:
            dims = ((1,), (0,)) if transposed else ((1,), (1,))
            added = lax.dot_general(block, w_ref[...], (dims, ((), ())), preferred_element_type=F32)
            if part == 1:
                total[...] += added
            elif has_total:
                total[...] = total_in[...] + added
            else:
                total[...] = added

    for part, ref in enumerate((a_ref, b_ref)):
        pl.when(pl.program_id(0) == part)(functools.partial(step, ref, part))


def consume(a, b, w, y, me, transposed, first, total=None, grad=None, wants=("total", "grad")):
    tokens, depth = y.shape
    block = (EIGHT, tokens, CHUNK)
    whole = lambda i, me: (0, 0)
    chunks = pl.BlockSpec(block, lambda i, me: (0, 0, 0))
    weights = weight_spec(transposed, depth, first, lambda i: i)
    in_specs, operands = [chunks, chunks], [me, a, b]
    out_specs, out_shape, aliases = [], [], {}
    if "total" in wants:
        in_specs.append(weights)
        operands.append(w)
        out_specs.append(pl.BlockSpec((tokens, depth), whole))
        out_shape.append(jax.ShapeDtypeStruct((tokens, depth), F32))
    if "grad" in wants:
        in_specs.append(pl.BlockSpec(y.shape, whole))
        operands.append(y)
        out_specs.append(weights)
        out_shape.append(jax.ShapeDtypeStruct(w.shape, BF16))
    if total is not None:
        aliases[len(operands)] = 0
        in_specs.append(pl.BlockSpec((tokens, depth), whole))
        operands.append(total)
    if grad is not None:
        aliases[len(operands)] = len(out_shape) - 1
        in_specs.append(pl.BlockSpec(memory_space=pl.ANY))
        operands.append(grad)
    return pl.pallas_call(
        functools.partial(consume_body, transposed, total is not None, grad is not None, wants),
        out_shape=out_shape,
        grid_spec=pltpu.PrefetchScalarGridSpec(
            num_scalar_prefetch=1, grid=(2,), in_specs=in_specs, out_specs=out_specs
        ),
        input_output_aliases=aliases,
        compiler_params=pltpu.CompilerParams(vmem_limit_bytes=LIMIT),
        cost_estimate=pl.CostEstimate(
            flops=4 * tokens * depth * CHUNK,
            bytes_accessed=tokens * depth,
            transcendentals=0,
        ),
    )(*operands)


def add(*terms):
    total = terms[0].astype(F32)
    for term in terms[1:]:
        total = total + term.astype(F32)
    return total


def after(value, *others):
    return lax.optimization_barrier((value,) + others)[0]


def join(block, got):
    return jnp.concatenate([block, got], axis=0)


def gather_rows(normed, d_out):
    normed = join(normed, send(normed, FIRST_Z))
    d_out = join(d_out, send(d_out, FIRST_Z))
    normed = join(normed, send(normed, SECOND_Z))
    got = send(after(d_out, normed), SECOND_Z)
    normed = join(normed, send(normed, CORES))
    return normed, (d_out, got)


def stage(values, *earlier):
    values, unused = lax.optimization_barrier((values, earlier))
    return values


def fuse(blocks):
    blocks = [block.astype(BF16) for block in blocks]
    return blocks[0] if len(blocks) == 1 else jnp.stack(blocks)


def split(block, count):
    return [block] if count == 1 else [block[n] for n in range(count)]


def scatter_rows(totals):
    count = len(totals)
    half = totals[0].shape[0] // 2
    got = split(send(fuse([total[half:] for total in totals]), CORES), count)
    totals = [add(total[:half], other) for total, other in zip(totals, got)]
    rows = half // 4
    kept = [total[:rows] for total in totals]
    sent = [fuse([total[rows * n : rows * (n + 1)] for total in totals]) for n in range(1, 4)]
    got = [
        split(send(block, perm), count)
        for block, perm in zip(sent, (FIRST_Z, SECOND_Z, ACROSS_Z))
    ]
    return [add(kept[n], *[g[n] for g in got]).astype(BF16) for n in range(count)], sent


def halve_first(x, w, me, transposed):
    far = [produce(x, w, me, transposed, (h,), 1)[0] for h in range(2)]
    got = [send(far[h], PRIMARY[h]) for h in range(2)]
    near = produce(x, w, me, transposed, (0, 1), 0)
    return near, got


def halve_second(near, got):
    out = [send(add(near[h][4:], got[h][4:]).astype(BF16), PRIMARY[1 - h]) for h in range(2)]
    return [add(near[h][:4], got[h][:4], out[h]) for h in range(2)]


def exchange(four):
    own = jnp.stack([four[0][0], four[1][0]])
    last = [
        send(jnp.stack([four[0][k], four[1][k]]).astype(BF16), SECONDARY[k]) for k in (1, 3, 2)
    ]
    return add(own, *last)


def spread_first(own):
    one, three, two = (send(own, SECONDARY[k]) for k in (1, 3, 2))
    return [jnp.stack([own[h], one[h], two[h], three[h]]) for h in range(2)]


def spread_second(four):
    return [
        jnp.concatenate([four[h], send(four[h], PRIMARY[1 - h])], axis=0) for h in range(2)
    ]


def spread_third(near):
    return [send(near[h], PRIMARY[h]) for h in range(2)]


def shards(normed, w_in, w_out, d_out):
    me = places()
    inputs, rows = gather_rows(normed, d_out)
    p_out = [produce(inputs, w_in, me, False, (0,), 1)[0]]
    cotangent = join(*rows)
    cotangent = join(cotangent, send(cotangent, CORES))
    p_out.append(produce(inputs, w_in, me, False, (1,), 1)[0])
    p_got = [send(p_out[h], PRIMARY[h]) for h in range(2)]
    p_near = produce(inputs, w_in, me, False, (0, 1), 0)
    d_near, d_got = halve_first(cotangent, w_out, me, True)
    p_four = halve_second(p_near, p_got)
    d_four = halve_second(d_near, d_got)
    preact = exchange(p_four)
    d_act = exchange(d_four)
    act = gelu_tanh(preact).astype(BF16)
    act, preact = lax.optimization_barrier((act, preact))
    p_four = spread_first(act)
    d_pre = (d_act * gelu_slope(preact)).astype(BF16)
    p_near = spread_second(p_four)
    d_four = spread_first(d_pre)
    p_far = spread_third(p_near)
    d_near = spread_second(d_four)
    total, grad = consume(p_near[0], p_near[1], w_out, cotangent, me, True, 0)
    d_far = spread_third([after(d_near[h], total) for h in range(2)])
    d_total, d_grad = consume(d_near[0], d_near[1], w_in, inputs, me, False, 0)
    p_far[0] = after(p_far[0], d_total)
    total, grad_out = consume(p_far[0], p_far[1], w_out, cotangent, me, True, 1, total, grad)
    (d_total,) = consume(d_far[0], d_far[1], w_in, inputs, me, False, 1, d_total, None, ("total",))
    (ffn_out, d_normed), sent = scatter_rows([total, d_total])
    d_far = stage(d_far, d_total, sent)
    (grad_in,) = consume(d_far[0], d_far[1], w_in, inputs, me, False, 1, None, d_grad, ("grad",))
    return (ffn_out, d_normed, grad_in, grad_out)


def solution(mesh):
    return jax.shard_map(
        shards,
        mesh=mesh,
        in_specs=(P("row", "col"), P("col", "row"), P("row", "col"), P("row", "col")),
        out_specs=(P("row", "col"), P("row", "col"), P("col", "row"), P("row", "col")),
        check_vma=False,
    )
```

```python
import functools

import jax
import jax.numpy as jnp
from jax import lax
from jax.experimental import pallas as pl
from jax.experimental.pallas import tpu as pltpu
from jax.sharding import PartitionSpec as P

BOTH = ("row", "col")
F32, BF16 = jnp.float32, jnp.bfloat16
CHUNK = 128
EIGHT = 8
LIMIT = 20 * 1024 * 1024


def gelu_tanh(value):
    inner = 0.7978845608 * (value + 0.044715 * value * value * value)
    return 0.5 * value * (1.0 + jnp.tanh(inner))


def gelu_slope(value):
    tangent = jnp.tanh(0.7978845608 * (value + 0.044715 * value * value * value))
    return 0.5 * (1.0 + tangent) + 0.5 * value * (1.0 - tangent * tangent) * 0.7978845608 * (
        1.0 + 3.0 * 0.044715 * value * value
    )


GRAY = (0, 1, 3, 2)
UNGRAY = (0, 1, 3, 2)


def pairs(move):
    listed = []
    for z in range(4):
        for core in range(2):
            for y in range(4):
                for x in range(4):
                    tz, tcore, ty, tx = move(z, core, y, x)
                    listed.append(
                        ((z * 2 + core) * 16 + y * 4 + x, (tz * 2 + tcore) * 16 + ty * 4 + tx)
                    )
    return listed


def flip(position, bit):
    return UNGRAY[GRAY[position] ^ (1 << bit)]


PRIMARY = [
    pairs(
        lambda z, core, y, x, bit=bit: (z, core, y, flip(x, bit))
        if core == 0
        else (z, core, flip(y, bit), x)
    )
    for bit in range(2)
]
SECONDARY = [
    pairs(lambda z, core, y, x, k=k: (z, core, y ^ k, x) if core == 0 else (z, core, y, x ^ k))
    for k in range(4)
]
FIRST_Z, SECOND_Z = (
    pairs(lambda z, core, y, x, turn=turn: (flip(z, core ^ turn), core, y, x)) for turn in range(2)
)
ACROSS_Z = pairs(lambda z, core, y, x: (z ^ 2, core, y, x))
CORES = pairs(lambda z, core, y, x: (z, 1 - core, y, x))


def send(block, perm):
    return lax.ppermute(block, BOTH, perm)


def gray(position):
    return jnp.bitwise_xor(position, jnp.right_shift(position, 1))


def places():
    row, col = lax.axis_index("row"), lax.axis_index("col")
    core, y, x = row % 2, col // 4, col % 4
    primary = gray(jnp.where(core == 0, x, y))
    secondary = jnp.where(core == 0, y, x)
    low, high = primary % 2, primary // 2
    return jnp.stack([low * 8 + high * 4 + secondary, high * 8 + low * 4 + secondary]).astype(
        jnp.int32
    )


def order(me, part, count):
    return [jnp.bitwise_xor(chunk, me[part] % count) for chunk in range(count)]


def weight_spec(transposed, depth, first, part_of):
    def index(i, me):
        part = part_of(i)
        group = jnp.bitwise_xor(first, jnp.right_shift(me[part], 3)) + 2 * part
        return (group, 0) if transposed else (0, group)

    wide = EIGHT * CHUNK
    return pl.BlockSpec((wide, depth) if transposed else (depth, wide), index)


def produce_body(transposed, parts, me, x_ref, w_ref, *outs):
    if transposed:
        term = lax.dot_general(
            x_ref[...], w_ref[...], (((1,), (1,)), ((), ())), preferred_element_type=F32
        )
    else:
        term = jnp.dot(x_ref[...], w_ref[...], preferred_element_type=F32)
    term = term.astype(BF16)

    def put(out, part):
        for chunk, place in enumerate(order(me, part, EIGHT)):
            out[place] = term[:, CHUNK * chunk : CHUNK * (chunk + 1)]

    if len(parts) == 1:
        put(outs[0], parts[0])
    else:
        for n, part in enumerate(parts):
            pl.when(pl.program_id(0) == n)(functools.partial(put, outs[n], part))


def produce(x, w, me, transposed, parts, first):
    tokens, depth = x.shape
    count = len(parts)
    part_of = (lambda i: parts[0]) if count == 1 else (lambda i: i)
    block = (EIGHT, tokens, CHUNK)
    return pl.pallas_call(
        functools.partial(produce_body, transposed, parts),
        out_shape=[jax.ShapeDtypeStruct(block, BF16)] * count,
        grid_spec=pltpu.PrefetchScalarGridSpec(
            num_scalar_prefetch=1,
            grid=(count,),
            in_specs=[
                pl.BlockSpec((tokens, depth), lambda i, me: (0, 0)),
                weight_spec(transposed, depth, first, part_of),
            ],
            out_specs=[pl.BlockSpec(block, lambda i, me: (0, 0, 0))] * count,
        ),
        compiler_params=pltpu.CompilerParams(vmem_limit_bytes=LIMIT),
        cost_estimate=pl.CostEstimate(
            flops=tokens * depth * CHUNK * count,
            bytes_accessed=tokens * depth,
            transcendentals=0,
        ),
    )(me, x, w)


def consume_body(transposed, has_total, has_grad, wants, me, a_ref, b_ref, *rest):
    rest = list(rest)
    w_ref = rest.pop(0) if "total" in wants else None
    y_ref = rest.pop(0) if "grad" in wants else None
    total_in = rest.pop(0) if has_total else None
    if has_grad:
        rest.pop(0)
    total = rest.pop(0) if "total" in wants else None
    grad = rest.pop(0) if "grad" in wants else None

    def step(ref, part):
        block = jnp.concatenate([ref[place] for place in order(me, part, EIGHT)], axis=1)
        if grad is not None and transposed:
            grad[...] = lax.dot_general(
                block, y_ref[...], (((0,), (0,)), ((), ())), preferred_element_type=F32
            ).astype(BF16)
        elif grad is not None:
            grad[...] = lax.dot_general(
                y_ref[...], block, (((0,), (0,)), ((), ())), preferred_element_type=F32
            ).astype(BF16)
        if total is not None:
            dims = ((1,), (0,)) if transposed else ((1,), (1,))
            added = lax.dot_general(block, w_ref[...], (dims, ((), ())), preferred_element_type=F32)
            if part == 1:
                total[...] += added
            elif has_total:
                total[...] = total_in[...] + added
            else:
                total[...] = added

    for part, ref in enumerate((a_ref, b_ref)):
        pl.when(pl.program_id(0) == part)(functools.partial(step, ref, part))


def consume(a, b, w, y, me, transposed, first, total=None, grad=None, wants=("total", "grad")):
    tokens, depth = y.shape
    block = (EIGHT, tokens, CHUNK)
    whole = lambda i, me: (0, 0)
    chunks = pl.BlockSpec(block, lambda i, me: (0, 0, 0))
    weights = weight_spec(transposed, depth, first, lambda i: i)
    in_specs, operands = [chunks, chunks], [me, a, b]
    out_specs, out_shape, aliases = [], [], {}
    if "total" in wants:
        in_specs.append(weights)
        operands.append(w)
        out_specs.append(pl.BlockSpec((tokens, depth), whole))
        out_shape.append(jax.ShapeDtypeStruct((tokens, depth), F32))
    if "grad" in wants:
        in_specs.append(pl.BlockSpec(y.shape, whole))
        operands.append(y)
        out_specs.append(weights)
        out_shape.append(jax.ShapeDtypeStruct(w.shape, BF16))
    if total is not None:
        aliases[len(operands)] = 0
        in_specs.append(pl.BlockSpec((tokens, depth), whole))
        operands.append(total)
    if grad is not None:
        aliases[len(operands)] = len(out_shape) - 1
        in_specs.append(pl.BlockSpec(memory_space=pl.ANY))
        operands.append(grad)
    return pl.pallas_call(
        functools.partial(consume_body, transposed, total is not None, grad is not None, wants),
        out_shape=out_shape,
        grid_spec=pltpu.PrefetchScalarGridSpec(
            num_scalar_prefetch=1, grid=(2,), in_specs=in_specs, out_specs=out_specs
        ),
        input_output_aliases=aliases,
        compiler_params=pltpu.CompilerParams(vmem_limit_bytes=LIMIT),
        cost_estimate=pl.CostEstimate(
            flops=4 * tokens * depth * CHUNK,
            bytes_accessed=tokens * depth,
            transcendentals=0,
        ),
    )(*operands)


def add(*terms):
    total = terms[0].astype(F32)
    for term in terms[1:]:
        total = total + term.astype(F32)
    return total


def after(value, *others):
    return lax.optimization_barrier((value,) + others)[0]


def join(block, got):
    return jnp.concatenate([block, got], axis=0)


def gather_rows(normed, d_out):
    normed = join(normed, send(normed, FIRST_Z))
    d_out = join(d_out, send(d_out, FIRST_Z))
    normed = join(normed, send(normed, SECOND_Z))
    got = send(after(d_out, normed), SECOND_Z)
    normed = join(normed, send(normed, CORES))
    return normed, (d_out, got)


def stage(values, *earlier):
    values, unused = lax.optimization_barrier((values, earlier))
    return values


def fuse(blocks):
    blocks = [block.astype(BF16) for block in blocks]
    return blocks[0] if len(blocks) == 1 else jnp.stack(blocks)


def split(block, count):
    return [block] if count == 1 else [block[n] for n in range(count)]


def scatter_rows(totals):
    count = len(totals)
    half = totals[0].shape[0] // 2
    got = split(send(fuse([total[half:] for total in totals]), CORES), count)
    totals = [add(total[:half], other) for total, other in zip(totals, got)]
    rows = half // 4
    kept = [total[:rows] for total in totals]
    sent = [fuse([total[rows * n : rows * (n + 1)] for total in totals]) for n in range(1, 4)]
    got = [
        split(send(block, perm), count)
        for block, perm in zip(sent, (FIRST_Z, SECOND_Z, ACROSS_Z))
    ]
    return [add(kept[n], *[g[n] for g in got]).astype(BF16) for n in range(count)], sent


def halve_first(x, w, me, transposed):
    far = [produce(x, w, me, transposed, (h,), 1)[0] for h in range(2)]
    got = [send(far[h], PRIMARY[h]) for h in range(2)]
    near = produce(x, w, me, transposed, (0, 1), 0)
    return near, got


def halve_second(near, got):
    out = [send(add(near[h][4:], got[h][4:]).astype(BF16), PRIMARY[1 - h]) for h in range(2)]
    return [add(near[h][:4], got[h][:4], out[h]) for h in range(2)]


def exchange(four):
    own = jnp.stack([four[0][0], four[1][0]])
    last = [
        send(jnp.stack([four[0][k], four[1][k]]).astype(BF16), SECONDARY[k]) for k in (1, 3, 2)
    ]
    return add(own, *last)


def spread_first(own):
    one, three, two = (send(own, SECONDARY[k]) for k in (1, 3, 2))
    return [jnp.stack([own[h], one[h], two[h], three[h]]) for h in range(2)]


def spread_second(four):
    return [
        jnp.concatenate([four[h], send(four[h], PRIMARY[1 - h])], axis=0) for h in range(2)
    ]


def spread_third(near):
    return [send(near[h], PRIMARY[h]) for h in range(2)]


def shards(normed, w_in, w_out, d_out):
    me = places()
    inputs, rows = gather_rows(normed, d_out)
    p_out = [produce(inputs, w_in, me, False, (0,), 1)[0]]
    cotangent = join(*rows)
    cotangent = join(cotangent, send(cotangent, CORES))
    p_out.append(produce(inputs, w_in, me, False, (1,), 1)[0])
    p_got = [send(p_out[h], PRIMARY[h]) for h in range(2)]
    p_near = produce(inputs, w_in, me, False, (0, 1), 0)
    d_near, d_got = halve_first(cotangent, w_out, me, True)
    p_four = halve_second(p_near, p_got)
    d_four = halve_second(d_near, d_got)
    preact = exchange(p_four)
    d_act = exchange(d_four)
    act = gelu_tanh(preact).astype(BF16)
    act, preact = lax.optimization_barrier((act, preact))
    p_four = spread_first(act)
    d_pre = (d_act * gelu_slope(preact)).astype(BF16)
    p_near = spread_second(p_four)
    d_four = spread_first(d_pre)
    p_far = spread_third(p_near)
    d_near = spread_second(d_four)
    total, grad = consume(p_near[0], p_near[1], w_out, cotangent, me, True, 0)
    d_far = spread_third(d_near)
    d_total, d_grad = consume(d_near[0], d_near[1], w_in, inputs, me, False, 0)
    p_far[0] = after(p_far[0], d_total)
    total, grad_out = consume(p_far[0], p_far[1], w_out, cotangent, me, True, 1, total, grad)
    (d_total,) = consume(d_far[0], d_far[1], w_in, inputs, me, False, 1, d_total, None, ("total",))
    (ffn_out, d_normed), sent = scatter_rows([total, d_total])
    d_far = stage(d_far, d_total, sent)
    (grad_in,) = consume(d_far[0], d_far[1], w_in, inputs, me, False, 1, None, d_grad, ("grad",))
    return (ffn_out, d_normed, grad_in, grad_out)


def solution(mesh):
    return jax.shard_map(
        shards,
        mesh=mesh,
        in_specs=(P("row", "col"), P("col", "row"), P("row", "col"), P("row", "col")),
        out_specs=(P("row", "col"), P("row", "col"), P("col", "row"), P("row", "col")),
        check_vma=False,
    )
```
